32 devices in a mesh: dp: 2 (over core), wide: 8 (over z, y), narrow: 2 (over x).
Axes of the slice: x: 2, y: 2, z: 4, core: 2. Of those that a mesh axis runs over, the one named last changes fastest.
Arguments:
- tokens: bfloat16 [16384, 1280], P(('dp', 'wide'), 'narrow'), may hold values from -44 to 44
- documents: int32 [16, 1024], P(('dp', 'wide')), may hold values from 0 to 3, never falling along the last dimension, each value on 1 to 512 neighbouring positions
- first_gain: float32 [1280], P('narrow'), may hold values from 0.5 to 1.5
- first_shift: float32 [1280], P('narrow'), may hold values from -1.5 to 1.5
- input_weight: bfloat16 [1280, 3, 1280], P('wide', None, 'narrow'), may hold values from -0.15625 to 0.15625
- input_bias: float32 [2, 1280], P(None, 'narrow'), may hold values from -2 to 2
- output_weight: bfloat16 [1280, 1280], P('narrow', 'wide'), may hold values from -2 to 2
- output_bias: float32 [1280], P('narrow'), may hold values from -1.5 to 1.5
- second_gain: float32 [1280], P('narrow'), may hold values from 0.5 to 1.5
- second_shift: float32 [1280], P('narrow'), may hold values from -1.5 to 1.5
- expand_weight: bfloat16 [1280, 5120], P('wide', 'narrow'), may hold values from -0.15625 to 0.15625
- expand_bias: float32 [5120], P('narrow'), may hold values from -2.5 to 2.5
- reduce_weight: bfloat16 [5120, 1280], P('narrow', 'wide'), may hold values from -0.15625 to 0.15625
- reduce_bias: float32 [1280], P('narrow'), may hold values from -1.5 to 1.5
- cotangent: bfloat16 [16384, 1280], P(('dp', 'wide'), 'narrow'), may hold values from -6 to 6
Outputs:
- layer_output: bfloat16 [16384, 1280], P(('dp', 'wide'), 'narrow')
- grad_tokens: float32 [16384, 1280], P(('dp', 'wide'), 'narrow')
- grad_first_gain: float32 [1280], P('narrow')
- grad_first_shift: float32 [1280], P('narrow')
- grad_input_weight: float32 [1280, 3, 1280], P('wide', None, 'narrow')
- grad_input_bias: float32 [2, 1280], P(None, 'narrow')
- grad_output_weight: float32 [1280, 1280], P('narrow', 'wide')
- grad_output_bias: float32 [1280], P('narrow')
- grad_second_gain: float32 [1280], P('narrow')
- grad_second_shift: float32 [1280], P('narrow')
- grad_expand_weight: float32 [1280, 5120], P('wide', 'narrow')
- grad_expand_bias: float32 [5120], P('narrow')
- grad_reduce_weight: float32 [5120, 1280], P('narrow', 'wide')
- grad_reduce_bias: float32 [1280], P('narrow')
The draws below stay inside these ranges and needn't reach their ends.
Inputs may be any that keep to these rules, and one draw needn't show every extreme that they name: Each row numbers its 4 documents 0 to 3 in order, never falling; each document has 1 to 512 tokens and one has exactly 512.
All inputs are finite; a program needn't handle non-finite values.
Results may differ from the reference program's by a relative error of at most 0.019.
Values may be sent and summed in bfloat16 or wider, within the bound.
No kernel may reach another device: no remote copies, remote signals or barrier semaphores. Data moves between devices by JAX's collectives and lax.ppermute only.
A program may use at most 192 MiB of HBM per device.

```python
import math
import jax
import jax.numpy as jnp
import numpy as np
from jax import lax

D = 1280
HEADS = 20
FF = 5120
LEN = 1024
DOCS = 4
SEQUENCES = 16
TOKENS = 16384


def draw_tokens(key, part):
    key = jax.random.fold_in(key, 7)
    key_base, key_cols, key_rows = jax.random.split(key, 3)
    places = jnp.arange(D, dtype=jnp.float32) / max(D - 1, 1)
    col_scale = 3.0 ** (places - 0.5) * 10.0 ** (jax.random.uniform(key_cols, (D,), jnp.float32) - 0.5)
    row_scale = 2.0 ** (jax.random.uniform(key_rows, (TOKENS, 1), jnp.float32) * 2.0 - 1.0)
    base_values = jnp.clip(jax.random.normal(key_base, (TOKENS, D), jnp.float32), -4.0, 4.0) * row_scale
    return (base_values * col_scale).astype(jnp.bfloat16)


def raised(entries, own_key, source, target, parts, factor):
    owner, partner = [(jnp.arange(entries.shape[axis_at]) // (entries.shape[axis_at] // parts)).reshape([-1 if axis == axis_at else 1 for axis in range(entries.ndim)]) for axis_at in (source, target)]
    chosen = jax.random.permutation(own_key, parts)[partner]
    strong = (owner == chosen) | (owner == (partner + parts // 2) % parts)
    return jnp.where(strong, factor * entries, entries)


def level_of(key, dims, cuts, least, largest):
    def one(axis_at, blocks):
        heights = jax.random.uniform(jax.random.fold_in(jax.random.fold_in(key, 6), axis_at), (blocks,), jnp.float32, least / len(cuts), largest / len(cuts))
        return jnp.repeat(jnp.exp(heights), dims[axis_at] // blocks).reshape((-1,) + (1,) * (len(dims) - axis_at - 1))

    factor_of = one(*cuts[0])
    for cut in cuts[1:]:
        factor_of = factor_of * one(*cut)
    return factor_of


def split_up(amount, total, reach, slope):
    weights = [(1 << 20) // math.isqrt(rank ** slope) + 1 for rank in range(2, amount + 1)]
    spare, holding = total - reach - (amount - 1), [1] * (amount - 1)
    while spare > 0:
        candidates = [i for i in range(amount - 1) if holding[i] < reach]
        whole, left = sum([weights[i] for i in candidates]), spare
        for i in candidates:
            addition = min(reach - holding[i], max(1, left * weights[i] // whole), spare)
            holding[i] = holding[i] + addition
            spare = spare - addition
    return np.array([reach] + holding)


def uneven_parts(key, number_of, total, most, slope):
    if number_of == 2:
        one = jax.random.randint(key, (), max(1, total - most), min(most, total - 1) + 1)
        return jnp.stack([one, total - one])
    sizes = jnp.asarray(split_up(number_of, total, most, slope), jnp.int32)
    pairs = (number_of - 1) // 2
    source_of, taker = sizes[1:1 + 2 * pairs:2], sizes[2:2 + 2 * pairs:2]
    room = jnp.minimum(source_of - 1, most - taker)
    moved = jax.random.randint(jax.random.fold_in(key, 1), (pairs,), 0, 1 << 20) % (room + 1)
    sizes = sizes.at[1:1 + 2 * pairs:2].set(source_of - moved).at[2:2 + 2 * pairs:2].set(taker + moved)
    return sizes[jax.random.permutation(jax.random.fold_in(key, 2), number_of)]


def normal_values(key, extent, deviation, most, pieces=(), held_as=jnp.bfloat16):
    factor_of = level_of(key, extent, pieces, -0.22, 0.18) if pieces else 1.0
    array = jax.random.normal(key, extent, jnp.float32) * deviation * factor_of
    return jnp.minimum(jnp.maximum(array, -most), most).astype(held_as)


def gaussian_with(rng, dims, spread, reach, cuts, heavy, held_as=jnp.bfloat16):
    array = spread * jax.random.normal(rng, dims, jnp.float32)
    if cuts:
        array = array * level_of(rng, dims, cuts, -0.22, 0.18)
    return jnp.clip(raised(array, jax.random.fold_in(rng, 3), *heavy), -reach, reach).astype(held_as)


def setup_inputs(seed: int = 0) -> dict:
    streams_of = jax.random.split(jax.random.key(seed), 16)
    return {
        "tokens": draw_tokens(jax.random.fold_in(streams_of[15], 71), 0),
        "documents": jax.vmap(lambda own: jnp.searchsorted(jnp.cumsum(uneven_parts(own, DOCS, LEN, LEN // 2, 1)), jnp.arange(LEN), side="right"))(jax.random.split(streams_of[1], SEQUENCES)).reshape((SEQUENCES, LEN)).astype(jnp.int32),
        "first_gain": jnp.clip(1.0 + 0.1 * jax.random.normal(streams_of[2], (D,), jnp.float32), 0.5, 1.5),
        "first_shift": normal_values(streams_of[3], (D,), 0.3, 1.5, ((0, 2),), jnp.float32),
        "input_weight": normal_values(streams_of[4], (D, 3, D), D ** -0.5, 0.15625, ((0, 8), (2, 2))),
        "input_bias": normal_values(streams_of[5], (2, D), 0.4, 2.0, ((1, 2),), jnp.float32),
        "output_weight": normal_values(streams_of[6], (D, D), (max(D // 128, 1)) ** -0.5, 2.0, ((0, 2), (1, 8))),
        "output_bias": normal_values(streams_of[7], (D,), 0.3, 1.5, ((0, 2),), jnp.float32),
        "second_gain": jnp.clip(1.0 + 0.1 * jax.random.normal(streams_of[8], (D,), jnp.float32), 0.5, 1.5),
        "second_shift": normal_values(streams_of[9], (D,), 0.3, 1.5, ((0, 2),), jnp.float32),
        "expand_weight": normal_values(streams_of[10], (D, FF), D ** -0.5, 0.15625, ((0, 8), (1, 2))),
        "expand_bias": normal_values(streams_of[11], (FF,), 0.5, 2.5, ((0, 2),), jnp.float32),
        "reduce_weight": normal_values(streams_of[12], (FF, D), (FF // 4) ** -0.5, 0.15625, ((0, 2), (1, 8))),
        "reduce_bias": normal_values(streams_of[13], (D,), 0.3, 1.5, ((0, 2),), jnp.float32),
        "cotangent": gaussian_with(streams_of[14], (TOKENS, D), 1.0, 6.0, ((0, 16), (1, 2)), (0, 1, 16, 2.0)),
    }


@jax.custom_vjp
def low(v):
    return lax.optimization_barrier(v.astype(jnp.bfloat16)).astype(jnp.float32)

@jax.custom_vjp
def low_back(v):
    return v

def low_keep(v):
    return (low(v), None)

def low_pass(kept, grad):
    return (grad,)

def back_keep(v):
    return (v, None)

def back_low(kept, grad):
    return (low(grad),)
low.defvjp(low_keep, low_pass)
low_back.defvjp(back_keep, back_low)
highest = lax.Precision.HIGHEST

def layer_norm(values, norm_gain, norm_bias):
    row_mean = lax.optimization_barrier(jnp.mean(values, axis=-1, keepdims=True))
    centred = values - row_mean
    row_var = lax.optimization_barrier(jnp.mean(centred * centred, axis=-1, keepdims=True))
    return centred * lax.rsqrt(row_var + 1e-05) * norm_gain + norm_bias

def attend_sequence(packed):
    queries, all_keys, all_values, doc_row = packed
    head_dim = queries.shape[-1]
    scores = jnp.einsum('qhd,khd->hqk', queries, all_keys, precision=highest) * head_dim ** (-0.5)
    scores = low_back(scores)
    places = jnp.arange(queries.shape[0])
    allowed = (places[:, None] >= places[None, :]) & (doc_row[:, None] == doc_row[None, :])
    scores = jnp.where(allowed[None], scores, -1e+30)
    weights_low = low(jax.nn.softmax(scores, axis=-1))
    return jnp.einsum('hqk,khd->qhd', weights_low, all_values, precision=highest)

def layer_group(params, block_rows, doc_rows):
    first_gain, first_shift, input_weight, input_bias, output_weight, output_bias, second_gain, second_shift, expand_weight, expand_bias, reduce_weight, reduce_bias = params
    seq_count = doc_rows.shape[0]
    normed_one = low(layer_norm(block_rows, first_gain, first_shift))
    bias_all = jnp.stack([input_bias[0], jnp.zeros_like(input_bias[0]), input_bias[1]])
    projected = jnp.einsum('td,dcf->tcf', normed_one, input_weight, precision=highest) + bias_all
    projected = low(low_back(projected))
    reshaped = projected.reshape(seq_count, LEN, 3, HEADS, D // HEADS)
    attended = lax.map(jax.checkpoint(attend_sequence), (reshaped[:, :, 0], reshaped[:, :, 1], reshaped[:, :, 2], doc_rows))
    attended = low(low_back(attended.reshape(seq_count * LEN, D)))
    branch_one = low_back(jnp.dot(attended, output_weight, precision=highest) + output_bias)
    middle = block_rows + branch_one
    normed_two = low(layer_norm(middle, second_gain, second_shift))
    hidden = low_back(jnp.dot(normed_two, expand_weight, precision=highest) + expand_bias)
    active = low(jax.nn.gelu(hidden, approximate=True))
    branch_two = low_back(jnp.dot(active, reduce_weight, precision=highest) + reduce_bias)
    return middle + branch_two

def reference(tokens, documents, first_gain, first_shift, input_weight, input_bias, output_weight, output_bias, second_gain, second_shift, expand_weight, expand_bias, reduce_weight, reduce_bias, cotangent):
    group_size = math.gcd(SEQUENCES, max(1, 4096 // LEN))
    group_count = SEQUENCES // group_size

    def forward(block_all, *params):
        blocks = block_all.reshape(group_count, group_size * LEN, D)
        doc_blocks = documents.reshape(group_count, group_size, LEN)

        def one_group(packed):
            return layer_group(params, packed[0], packed[1])
        layer_out = lax.map(jax.checkpoint(one_group), (blocks, doc_blocks))
        return layer_out.reshape(TOKENS, D)
    floats = [arg.astype(jnp.float32) for arg in (tokens, first_gain, first_shift, input_weight, input_bias, output_weight, output_bias, second_gain, second_shift, expand_weight, expand_bias, reduce_weight, reduce_bias)]
    result, pull = jax.vjp(forward, *floats)
    grads = pull(cotangent.astype(jnp.float32))
    return (result.astype(jnp.bfloat16), grads[0], grads[1], grads[2], grads[3], grads[4], grads[5], grads[6], grads[7], grads[8], grads[9], grads[10], grads[11], grads[12])
```

```python
import jax
import jax.numpy as jnp
from jax import lax
from jax.sharding import PartitionSpec as P

D = 1280
HEADS = 20

epsilon = 1e-05
masked_value = -1e30

MESH = ("dp", "wide", "narrow")
PAIR = ("dp", "narrow")
f32 = jnp.float32
bf16 = jnp.bfloat16


def turn(values):
    return lax.ppermute(values, PAIR, [(0, 0), (1, 2), (2, 1), (3, 3)])


def core_swap(values):
    return lax.ppermute(values, "dp", [(0, 1), (1, 0)])


def side_swap(values):
    return lax.ppermute(values, "narrow", [(0, 1), (1, 0)])


def ring_order(size):
    return list(range(0, size, 2)) + list(range(size - 1, 0, -2))


def ring_place(index, size):
    return jnp.where(index % 2 == 0, index // 2, size - 1 - index // 2)


def ring_index(place, size):
    place = place % size
    return jnp.where(place < size // 2, 2 * place, 2 * (size - 1 - place) + 1)


def ring_step(values, shift, both):
    size = lax.axis_size("wide")
    order = ring_order(size)
    pairs = []
    for c in range(2):
        for n in range(2):
            if c != n and not both:
                continue
            for place in range(size):
                source = (c * size + order[place]) * 2 + n
                target = (c * size + order[(place + shift) % size]) * 2 + n
                pairs.append((source, target))
    return lax.ppermute(values, MESH, pairs)


def limits(size, flip):
    forward, backward = size // 2, size - 1 - size // 2
    if flip:
        forward, backward = backward, forward
    total = (size - 1) // 2
    near_forward = (total + 1) // 2 if forward >= backward else total // 2
    return ((1, forward, near_forward), (-1, backward, total - near_forward))


def same():
    return lax.axis_index("dp") == lax.axis_index("narrow")


def gather_rows(shard, flip=False):
    size = lax.axis_size("wide")
    rows = shard.shape[0]
    mine = turn(shard)
    me = lax.axis_index("wide")
    place = ring_place(me, size)
    whole = jnp.zeros((size * rows, shard.shape[1]), shard.dtype)
    whole = lax.dynamic_update_slice_in_dim(whole, mine, me * rows, 0)
    for shift, steps, near in limits(size, flip):
        current = mine
        for step in range(1, steps + 1):
            current = ring_step(current, shift, step <= near)
            chunk = current
            if step > near:
                across = lax.ppermute(current, PAIR, [(0, 1), (3, 2)])
                chunk = jnp.where(same(), current, across)
            owner = ring_index(place - shift * step, size)
            whole = lax.dynamic_update_slice_in_dim(whole, chunk, owner * rows, 0)
    return whole


def scatter_rows(partial, flip=False):
    size = lax.axis_size("wide")
    rows = partial.shape[0] // size
    me = lax.axis_index("wide")
    place = ring_place(me, size)

    def piece(offset):
        owner = ring_index(place + offset, size)
        return lax.dynamic_slice_in_dim(partial, owner * rows, rows, 0)

    total = piece(0).astype(f32)
    for shift, steps, near in limits(size, flip):
        moving = None
        for step in range(steps, 0, -1):
            term = piece(shift * step)
            if step > near:
                across = lax.ppermute(term, PAIR, [(1, 0), (2, 3)])
                term = term.astype(f32) + across.astype(f32)
            else:
                term = term.astype(f32)
            if moving is not None:
                term = term + jnp.where(same() | (step + 1 <= near), moving, 0).astype(f32)
            moving = ring_step(term.astype(bf16), shift, step <= near)
        total = total + moving.astype(f32)
    settled = turn(total.astype(bf16))
    return settled.astype(f32) + core_swap(settled).astype(f32)


def choose_half(own, other):
    first = lax.axis_index("dp") == 0
    axis = own.ndim - 1
    return jnp.where(
        first, jnp.concatenate([own, other], axis), jnp.concatenate([other, own], axis)
    )


def both_halves(values):
    return choose_half(values, core_swap(values))


def half_of(values, share, index):
    return lax.dynamic_slice_in_dim(values, index * share, share, values.ndim - 1)


def norm_parts(values):
    row_mean = jnp.mean(values, 1, keepdims=True)
    centred = values - row_mean
    row_var = jnp.mean(centred * centred, 1, keepdims=True)
    row_scale = lax.rsqrt(row_var + epsilon)
    return centred * row_scale, row_scale


def norm_backward(grad_in, standard, row_scale, norm_gain):
    scaled = grad_in * norm_gain
    plain = jnp.mean(scaled, 1, keepdims=True)
    cross = jnp.mean(scaled * standard, 1, keepdims=True)
    back = row_scale * (scaled - plain - standard * cross)
    return back, jnp.sum(grad_in * standard, 0), jnp.sum(grad_in, 0)


def dot_last(left, right):
    return lax.dot_general(left, right, (((1,), (1,)), ((), ())), preferred_element_type=f32)


def dot_first(left, right):
    return lax.dot_general(left, right, (((0,), (0,)), ((), ())), preferred_element_type=f32)


def dot(left, right):
    return jnp.dot(left, right, preferred_element_type=f32)


def masked_scores(queries, all_keys, doc_row, block_start, block_end):
    head_dim = queries.shape[-1]
    scores = jnp.einsum(
        "qhd,khd->hqk",
        queries[block_start:block_end],
        all_keys[:block_end],
        preferred_element_type=jnp.float32,
    ) * head_dim ** (-0.5)
    places = jnp.arange(block_end)
    allowed = (places[block_start:block_end, None] >= places[None, :]) & (
        doc_row[block_start:block_end, None] == doc_row[None, :block_end]
    )
    return jnp.where(allowed[None], scores, masked_value)


def attend(packed):
    queries, all_keys, all_values, doc_row = packed
    length = queries.shape[0]
    block_rows = min(512, length)
    out_blocks = []
    log_blocks = []
    for block_start in range(0, length, block_rows):
        block_end = block_start + block_rows
        scores = masked_scores(queries, all_keys, doc_row, block_start, block_end)
        row_top = jnp.max(scores, -1, keepdims=True)
        shifted_exp = jnp.exp(scores - row_top)
        denominator = jnp.sum(shifted_exp, -1, keepdims=True)
        softmax_low = (shifted_exp / denominator).astype(jnp.bfloat16)
        out_blocks.append(
            jnp.einsum(
                "hqk,khd->qhd",
                softmax_low,
                all_values[:block_end],
                preferred_element_type=jnp.float32,
            )
        )
        log_blocks.append((row_top + jnp.log(denominator))[..., 0])
    return (jnp.concatenate(out_blocks, 0), jnp.concatenate(log_blocks, 1))


def attend_backward(packed):
    queries, all_keys, all_values, doc_row, log_sums, grad_out = packed
    length = queries.shape[0]
    head_dim = queries.shape[-1]
    factor = head_dim ** (-0.5)
    block_rows = min(512, length)
    grad_keys = jnp.zeros(all_keys.shape, jnp.float32)
    grad_values = jnp.zeros(all_values.shape, jnp.float32)
    query_blocks = []
    for block_start in range(0, length, block_rows):
        block_end = block_start + block_rows
        scores = masked_scores(queries, all_keys, doc_row, block_start, block_end)
        softmax_rows = jnp.exp(scores - log_sums[:, block_start:block_end, None])
        grad_softmax = jnp.einsum(
            "qhd,khd->hqk",
            grad_out[block_start:block_end],
            all_values[:block_end],
            preferred_element_type=jnp.float32,
        )
        row_inner = jnp.sum(softmax_rows * grad_softmax, -1, keepdims=True)
        grad_scores = (softmax_rows * (grad_softmax - row_inner)).astype(jnp.bfloat16)
        query_blocks.append(
            jnp.einsum(
                "hqk,khd->qhd",
                grad_scores,
                all_keys[:block_end],
                preferred_element_type=jnp.float32,
            )
            * factor
        )
        grad_keys = grad_keys.at[:block_end].add(
            jnp.einsum(
                "hqk,qhd->khd",
                grad_scores,
                queries[block_start:block_end],
                preferred_element_type=jnp.float32,
            )
            * factor
        )
        grad_values = grad_values.at[:block_end].add(
            jnp.einsum(
                "hqk,qhd->khd",
                softmax_rows.astype(jnp.bfloat16),
                grad_out[block_start:block_end],
                preferred_element_type=jnp.float32,
            )
        )
    return (jnp.concatenate(query_blocks, 0), grad_keys, grad_values)


def gelu_tanh(values):
    return jax.nn.gelu(values, approximate=True)


def local(
    tokens,
    documents,
    first_gain,
    first_shift,
    input_weight,
    input_bias,
    output_weight,
    output_bias,
    second_gain,
    second_shift,
    expand_weight,
    expand_bias,
    reduce_weight,
    reduce_bias,
    cotangent,
):
    token_rows, share = tokens.shape
    seq_count, length = documents.shape
    head_dim = D // HEADS
    heads_here = share // head_dim
    hidden_here = expand_weight.shape[1]
    wide_rows = input_weight.shape[0]
    core = lax.axis_index("dp")
    side = lax.axis_index("narrow")

    input_rows = gather_rows(input_weight.reshape(wide_rows, 3 * share))
    small_sizes = [share] * 6 + [2 * share, hidden_here]
    small = jnp.concatenate(
        [
            first_gain,
            first_shift,
            output_bias,
            second_gain,
            second_shift,
            reduce_bias,
            input_bias.reshape(-1),
            expand_bias,
        ]
    )
    small_other = side_swap(small)
    small_low = jnp.where(side == 0, small, small_other)
    small_high = jnp.where(side == 0, small_other, small)

    def full_vector(k):
        at = k * share
        return jnp.concatenate([small_low[at : at + share], small_high[at : at + share]])

    own_half = jnp.where(core == 0, small_low, small_high)
    gain_one, shift_one, bias_out, gain_two, shift_two, bias_reduce = [
        full_vector(k) for k in range(6)
    ]
    bias_in = own_half[6 * share : 8 * share].reshape(2, share)
    bias_expand = own_half[8 * share :]
    docs = turn(documents)
    residual = both_halves(turn(tokens)).astype(f32)
    upstream_low = both_halves(turn(cotangent))
    output_t = gather_rows(output_weight.T, True)
    expand = gather_rows(expand_weight)
    reduce_t = gather_rows(reduce_weight.T, True)

    standard_one, scale_one = norm_parts(residual)
    normed_one = (standard_one * gain_one + shift_one).astype(bf16)
    bias_rows = jnp.stack([bias_in[0], jnp.zeros_like(bias_in[0]), bias_in[1]]).reshape(3 * share)
    projected = (dot(normed_one, input_rows) + bias_rows).astype(bf16)
    reshaped = projected.reshape(seq_count, length, 3, heads_here, head_dim)
    queries = reshaped[:, :, 0]
    all_keys = reshaped[:, :, 1]
    all_values = reshaped[:, :, 2]
    attended, log_sums = lax.map(attend, (queries, all_keys, all_values, docs))
    attended_low = attended.reshape(token_rows, share).astype(bf16)
    branch = dot_last(attended_low, output_t).astype(bf16)
    middle = residual + (branch.astype(f32) + core_swap(branch).astype(f32)) + bias_out
    standard_two, scale_two = norm_parts(middle)
    normed_two = (standard_two * gain_two + shift_two).astype(bf16)
    hidden = dot(normed_two, expand) + bias_expand
    active, gelu_pull = jax.vjp(gelu_tanh, hidden)
    active = active.astype(bf16)
    branch_two = dot_last(active, reduce_t).astype(bf16)
    branch_other = core_swap(half_of(branch_two, share, 1 - core))
    layer_output = (
        half_of(middle, share, core)
        + half_of(branch_two, share, core).astype(f32)
        + branch_other.astype(f32)
        + half_of(bias_reduce, share, core)
    ).astype(bf16)
    layer_output = turn(layer_output)

    grad_reduce_weight = scatter_rows(dot_first(upstream_low, active).astype(bf16), True).T
    upstream = upstream_low.astype(f32)
    grad_reduce_bias = jnp.sum(upstream, 0)
    grad_active = dot(upstream_low, reduce_t)
    grad_hidden = gelu_pull(grad_active)[0].astype(bf16)
    grad_expand_bias = jnp.sum(grad_hidden.astype(f32), 0)
    grad_expand_weight = scatter_rows(dot_first(normed_two, grad_hidden).astype(bf16))
    branch = dot_last(grad_hidden, expand).astype(bf16)
    grad_normed_two = branch.astype(f32) + core_swap(branch).astype(f32)
    grad_middle, grad_second_gain, grad_second_shift = norm_backward(
        grad_normed_two, standard_two, scale_two, gain_two
    )
    grad_middle = grad_middle + upstream
    grad_branch = grad_middle.astype(bf16)
    grad_output_bias = jnp.sum(grad_branch.astype(f32), 0)
    grad_attended = dot(grad_branch, output_t).astype(bf16)
    grad_output_weight = scatter_rows(dot_first(grad_branch, attended_low).astype(bf16), True).T
    grad_query, grad_key, grad_value = lax.map(
        attend_backward,
        (
            queries,
            all_keys,
            all_values,
            docs,
            log_sums,
            grad_attended.reshape(seq_count, length, heads_here, head_dim),
        ),
    )
    grad_projected = (
        jnp.stack([grad_query, grad_key, grad_value], 2)
        .reshape(token_rows, 3 * share)
        .astype(bf16)
    )
    projected_sums = jnp.sum(grad_projected.astype(f32), 0).reshape(3, share)
    grad_input_bias = jnp.stack([projected_sums[0], projected_sums[2]])
    grad_input_weight = scatter_rows(dot_first(normed_one, grad_projected).astype(bf16))
    branch = dot_last(grad_projected, input_rows).astype(bf16)
    grad_normed_one = branch.astype(f32) + core_swap(branch).astype(f32)
    grad_tokens, grad_first_gain, grad_first_shift = norm_backward(
        grad_normed_one, standard_one, scale_one, gain_one
    )
    grad_tokens = half_of(grad_tokens + grad_middle, share, core)
    grad_tokens = turn(grad_tokens.astype(bf16)).astype(f32)

    def placed(values):
        blank = jnp.zeros(values.shape[:-1] + (2 * values.shape[-1],), f32)
        return lax.dynamic_update_slice_in_dim(
            blank, values, core * values.shape[-1], values.ndim - 1
        )

    def own(values):
        return placed(half_of(values, share, core))

    sums = lax.psum(
        (
            own(grad_first_gain),
            own(grad_first_shift),
            placed(grad_input_bias),
            own(grad_output_bias),
            own(grad_second_gain),
            own(grad_second_shift),
            placed(grad_expand_bias),
            own(grad_reduce_bias),
        ),
        MESH,
    )
    sums = [half_of(value, value.shape[-1] // 2, side) for value in sums]
    return (
        layer_output,
        grad_tokens,
        sums[0],
        sums[1],
        grad_input_weight.reshape(-1, 3, share),
        sums[2],
        grad_output_weight,
        sums[3],
        sums[4],
        sums[5],
        grad_expand_weight,
        sums[6],
        grad_reduce_weight,
        sums[7],
    )


def solution(mesh):
    in_specs = (
        P(("dp", "wide"), "narrow"),
        P(("dp", "wide"), None),
        P("narrow"),
        P("narrow"),
        P("wide", None, "narrow"),
        P(None, "narrow"),
        P("narrow", "wide"),
        P("narrow"),
        P("narrow"),
        P("narrow"),
        P("wide", "narrow"),
        P("narrow"),
        P("narrow", "wide"),
        P("narrow"),
        P(("dp", "wide"), "narrow"),
    )
    out_specs = (
        P(("dp", "wide"), "narrow"),
        P(("dp", "wide"), "narrow"),
        P("narrow"),
        P("narrow"),
        P("wide", None, "narrow"),
        P(None, "narrow"),
        P("narrow", "wide"),
        P("narrow"),
        P("narrow"),
        P("narrow"),
        P("wide", "narrow"),
        P("narrow"),
        P("narrow", "wide"),
        P("narrow"),
    )
    return jax.shard_map(local, mesh=mesh, in_specs=in_specs, out_specs=out_specs, check_vma=False)
```

```python
import functools

import jax
import jax.numpy as jnp
from jax import lax
from jax.experimental import pallas as pl
from jax.experimental.pallas import tpu as pltpu
from jax.sharding import PartitionSpec as P

D = 1280
HEADS = 20

epsilon = 1e-05

MESH = ("dp", "wide", "narrow")
PAIR = ("dp", "narrow")
f32 = jnp.float32
bf16 = jnp.bfloat16


def turn(values):
    return lax.ppermute(values, PAIR, [(0, 0), (1, 2), (2, 1), (3, 3)])


def core_swap(values):
    return lax.ppermute(values, "dp", [(0, 1), (1, 0)])


def side_swap(values):
    return lax.ppermute(values, "narrow", [(0, 1), (1, 0)])


def after(values, *earlier):
    return lax.optimization_barrier((values,) + earlier)[0]


def ring_order(size):
    return list(range(0, size, 2)) + list(range(size - 1, 0, -2))


def ring_place(index, size):
    return jnp.where(index % 2 == 0, index // 2, size - 1 - index // 2)


def ring_index(place, size):
    place = place % size
    return jnp.where(place < size // 2, 2 * place, 2 * (size - 1 - place) + 1)


def ring_step(values, shift):
    size = lax.axis_size("wide")
    order = ring_order(size)
    pairs = [(order[p], order[(p + shift) % size]) for p in range(size)]
    return lax.ppermute(values, "wide", pairs)


def ring_owner(offset):
    size = lax.axis_size("wide")
    return ring_index(ring_place(lax.axis_index("wide"), size) + offset, size)


def ring_chunks(mine, flip=False):
    size = lax.axis_size("wide")
    ahead, behind = mine, mine
    rounds = [[(0, mine)]]
    sign = -1 if flip else 1
    for step in range(1, size // 2 + 1):
        ahead = ring_step(ahead, sign)
        rounds.append([(-sign * step, ahead)])
        if step < size - size // 2:
            behind = ring_step(behind, -sign)
            rounds[-1].append((sign * step, behind))
    return rounds


def gather_ring(mine, flip=False):
    rows = mine.shape[0]
    whole = jnp.zeros((lax.axis_size("wide") * rows, mine.shape[1]), mine.dtype)
    for arrived in ring_chunks(mine, flip):
        for offset, chunk in arrived:
            whole = lax.dynamic_update_slice_in_dim(whole, chunk, ring_owner(offset) * rows, 0)
    return whole


def gather_both(mine, flip=False):
    rows, columns = mine.shape
    side = lax.axis_index("narrow")
    whole = jnp.zeros((2, lax.axis_size("wide") * rows, columns), mine.dtype)
    rounds = ring_chunks(mine, flip)
    rounds = [rounds[0] + rounds[1]] + rounds[2:]
    for arrived in rounds:
        chunks = jnp.concatenate([chunk for _, chunk in arrived], 0) if len(arrived) > 1 else arrived[0][1]
        across = side_swap(chunks)
        for k, (offset, chunk) in enumerate(arrived):
            at = ring_owner(offset) * rows
            other = across[k * rows : (k + 1) * rows]
            whole = lax.dynamic_update_slice(whole, chunk[None], (side, at, 0))
            whole = lax.dynamic_update_slice(whole, other[None], (1 - side, at, 0))
    return whole


def scatter_ring(piece, flip=False):
    size = lax.axis_size("wide")
    sign = -1 if flip else 1
    total = piece(0)
    for shift, steps in ((sign, size // 2), (-sign, size - size // 2 - 1)):
        moving = None
        for step in range(steps, 0, -1):
            term = piece(shift * step)
            if moving is not None:
                term = term + moving.astype(f32)
            moving = ring_step(term.astype(bf16), shift)
        total = total + moving.astype(f32)
    return total


def scatter_half(partial, flip=False):
    rows = partial.shape[0] // lax.axis_size("wide")

    def piece(offset):
        return lax.dynamic_slice_in_dim(partial, ring_owner(offset) * rows, rows, 0).astype(f32)

    settled = turn(scatter_ring(piece, flip).astype(bf16))
    return settled.astype(f32) + core_swap(settled).astype(f32)


def scatter_both(partial, flip=False):
    size = lax.axis_size("wide")
    rows = partial.shape[1] // size
    side = lax.axis_index("narrow")
    sign = -1 if flip else 1
    pieces = {}

    def part(which, offset):
        at = ring_owner(offset) * rows
        return lax.dynamic_slice(partial, (which, at, 0), (1, rows, partial.shape[2]))[0]

    for step in range(size // 2, 0, -1):
        offsets = [sign * step, -sign * (step - 1)]
        across = side_swap(jnp.concatenate([part(1 - side, offset) for offset in offsets], 0))
        for k, offset in enumerate(offsets):
            mine = part(side, offset).astype(f32)
            pieces[offset] = mine + across[k * rows : (k + 1) * rows].astype(f32)
    return scatter_ring(lambda offset: pieces[offset], flip)


def choose_half(own, other):
    first = lax.axis_index("dp") == 0
    axis = own.ndim - 1
    return jnp.where(
        first, jnp.concatenate([own, other], axis), jnp.concatenate([other, own], axis)
    )


def both_halves(values):
    return choose_half(values, core_swap(values))


def half_of(values, share, index):
    return lax.dynamic_slice_in_dim(values, index * share, share, values.ndim - 1)


def all_sum(values):
    size = lax.axis_size("wide")
    if size & (size - 1):
        return lax.psum(values, MESH)
    total = values + core_swap(values)
    total = total + side_swap(total)
    step = 1
    while step < size:
        total = total + lax.ppermute(total, "wide", [(k, k ^ step) for k in range(size)])
        step *= 2
    return total


def norm_parts(values):
    row_mean = jnp.mean(values, 1, keepdims=True)
    centred = values - row_mean
    row_var = jnp.mean(centred * centred, 1, keepdims=True)
    row_scale = lax.rsqrt(row_var + epsilon)
    return centred * row_scale, row_scale


def norm_backward(grad_in, standard, row_scale, norm_gain):
    scaled = grad_in * norm_gain
    plain = jnp.mean(scaled, 1, keepdims=True)
    cross = jnp.mean(scaled * standard, 1, keepdims=True)
    back = row_scale * (scaled - plain - standard * cross)
    return back, jnp.sum(grad_in * standard, 0), jnp.sum(grad_in, 0)


def dot_last(left, right):
    return lax.dot_general(left, right, (((1,), (1,)), ((), ())), preferred_element_type=f32)


def dot_first(left, right):
    return lax.dot_general(left, right, (((0,), (0,)), ((), ())), preferred_element_type=f32)


def dot(left, right):
    return jnp.dot(left, right, preferred_element_type=f32)


def gelu_parts(hidden):
    slope = (2.0 / 3.141592653589793) ** 0.5
    square = hidden * hidden
    bent = jnp.tanh(slope * hidden * (1.0 + 0.044715 * square))
    half = 0.5 * (1.0 + bent)
    rate = half + 0.5 * hidden * (1.0 - bent * bent) * (slope * (1.0 + 0.134145 * square))
    return hidden * half, rate


masked_value = -1e30
BLOCK = 256
REACH = 512


def key_range(block, block_rows):
    first = max(0, (block * block_rows - (REACH - 1)) // block_rows * block_rows)
    return first, (block + 1) * block_rows


def seen(starts, first, last, query_at, rows):
    keys = lax.broadcasted_iota(jnp.int32, (last - first, rows), 0) + first
    queries = lax.broadcasted_iota(jnp.int32, (last - first, rows), 1) + query_at
    return (keys <= queries) & (keys >= starts)


def attend_kernel(starts_ref, packed_ref, out_ref, logs_ref, *, head_dim):
    length = packed_ref.shape[0]
    group = out_ref.shape[1]
    rows = min(BLOCK, length)
    factor = head_dim**-0.5
    for block in range(length // rows):
        first, last = key_range(block, rows)
        at = block * rows
        allowed = seen(starts_ref[0, :, at : at + rows], first, last, at, rows)
        outs = []
        for head in range(group // head_dim):
            low = head * head_dim
            query = packed_ref[at : at + rows, low : low + head_dim] * bf16(factor)
            key = packed_ref[first:last, group + low : group + low + head_dim]
            value = packed_ref[first:last, 2 * group + low : 2 * group + low + head_dim]
            scores = lax.dot_general(key, query, (((1,), (1,)), ((), ())), preferred_element_type=f32)
            scores = jnp.where(allowed, scores, masked_value)
            top = jnp.max(scores, 0, keepdims=True)
            raised = jnp.exp(scores - top)
            total = jnp.sum(raised, 0, keepdims=True)
            mixed = lax.dot_general(
                value, raised.astype(bf16), (((0,), (0,)), ((), ())), preferred_element_type=f32
            )
            outs.append(mixed / total)
            logs_ref[0, 0, head : head + 1, at : at + rows] = top + jnp.log(total)
        out_ref[at : at + rows, :] = jnp.concatenate(outs, 0).T.astype(bf16)


def attend_backward_kernel(
    starts_ref, packed_ref, logs_ref, grad_ref, out_ref, keys_scr, values_scr, *, head_dim
):
    length = packed_ref.shape[0]
    group = grad_ref.shape[1]
    rows = min(BLOCK, length)
    factor = head_dim**-0.5
    keys_scr[...] = jnp.zeros_like(keys_scr)
    values_scr[...] = jnp.zeros_like(values_scr)
    for block in range(length // rows):
        first, last = key_range(block, rows)
        at = block * rows
        allowed = seen(starts_ref[0, :, at : at + rows], first, last, at, rows)
        queries_back = []
        keys_back = []
        values_back = []
        for head in range(group // head_dim):
            low = head * head_dim
            query = packed_ref[at : at + rows, low : low + head_dim] * bf16(factor)
            key = packed_ref[first:last, group + low : group + low + head_dim]
            value = packed_ref[first:last, 2 * group + low : 2 * group + low + head_dim]
            grad = grad_ref[at : at + rows, low : low + head_dim]
            scores = lax.dot_general(key, query, (((1,), (1,)), ((), ())), preferred_element_type=f32)
            logs = logs_ref[0, 0, head : head + 1, at : at + rows]
            probs = jnp.exp(jnp.where(allowed, scores, masked_value) - logs)
            grad_probs = lax.dot_general(
                value, grad, (((1,), (1,)), ((), ())), preferred_element_type=f32
            )
            inner = jnp.sum(probs * grad_probs, 0, keepdims=True)
            grad_scores = (probs * (grad_probs - inner)).astype(bf16)
            queries_back.append(
                lax.dot_general(key, grad_scores, (((0,), (0,)), ((), ())), preferred_element_type=f32)
            )
            keys_back.append(jnp.dot(grad_scores, query, preferred_element_type=f32))
            values_back.append(jnp.dot(probs.astype(bf16), grad, preferred_element_type=f32))
        out_ref[at : at + rows, :group] = (jnp.concatenate(queries_back, 0).T * factor).astype(bf16)
        keys_scr[first:last, :] += jnp.concatenate(keys_back, 1)
        values_scr[first:last, :] += jnp.concatenate(values_back, 1)
    out_ref[:, group : 2 * group] = keys_scr[...].astype(bf16)
    out_ref[:, 2 * group :] = values_scr[...].astype(bf16)


def attend(packed, starts, group, head_dim):
    seq_count, _, length = starts.shape
    groups = packed.shape[1] // (3 * group)
    heads = group // head_dim
    return pl.pallas_call(
        functools.partial(attend_kernel, head_dim=head_dim),
        grid=(seq_count, groups),
        in_specs=[
            pl.BlockSpec((1, 1, length), lambda s, g: (s, 0, 0)),
            pl.BlockSpec((length, 3 * group), lambda s, g: (s, g)),
        ],
        out_specs=[
            pl.BlockSpec((length, group), lambda s, g: (s, g)),
            pl.BlockSpec((1, 1, heads, length), lambda s, g: (s, g, 0, 0)),
        ],
        out_shape=[
            jax.ShapeDtypeStruct((packed.shape[0], groups * group), bf16),
            jax.ShapeDtypeStruct((seq_count, groups, heads, length), f32),
        ],
        compiler_params=pltpu.CompilerParams(vmem_limit_bytes=48 * 1024 * 1024),
        cost_estimate=pl.CostEstimate(flops=12 * 10**9, bytes_accessed=6 * 10**6, transcendentals=0),
        name="attend",
    )(starts, packed)


def attend_backward(packed, starts, logs, grad, group, head_dim):
    seq_count, _, length = starts.shape
    groups = packed.shape[1] // (3 * group)
    heads = group // head_dim
    return pl.pallas_call(
        functools.partial(attend_backward_kernel, head_dim=head_dim),
        grid=(seq_count, groups),
        in_specs=[
            pl.BlockSpec((1, 1, length), lambda s, g: (s, 0, 0)),
            pl.BlockSpec((length, 3 * group), lambda s, g: (s, g)),
            pl.BlockSpec((1, 1, heads, length), lambda s, g: (s, g, 0, 0)),
            pl.BlockSpec((length, group), lambda s, g: (s, g)),
        ],
        out_specs=pl.BlockSpec((length, 3 * group), lambda s, g: (s, g)),
        out_shape=jax.ShapeDtypeStruct(packed.shape, bf16),
        scratch_shapes=[pltpu.VMEM((length, group), f32), pltpu.VMEM((length, group), f32)],
        compiler_params=pltpu.CompilerParams(vmem_limit_bytes=48 * 1024 * 1024),
        cost_estimate=pl.CostEstimate(flops=30 * 10**9, bytes_accessed=10 * 10**6, transcendentals=0),
        name="attend_backward",
    )(starts, packed, logs, grad)


def local(
    tokens,
    documents,
    first_gain,
    first_shift,
    input_weight,
    input_bias,
    output_weight,
    output_bias,
    second_gain,
    second_shift,
    expand_weight,
    expand_bias,
    reduce_weight,
    reduce_bias,
    cotangent,
):
    token_rows, share = tokens.shape
    head_dim = D // HEADS
    group = 2 * head_dim
    groups = share // group
    hidden_half = expand_weight.shape[1]
    part_here = hidden_half // 2
    wide_rows = input_weight.shape[0]
    wide_size = lax.axis_size("wide")
    core = lax.axis_index("dp")
    side = lax.axis_index("narrow")

    input_rows = input_weight.reshape(wide_rows, 3, groups, group).transpose(0, 2, 1, 3)
    input_rows = turn(input_rows.reshape(wide_rows, 3 * share))
    input_all = gather_ring(input_rows)
    output_all = gather_ring(after(turn(output_weight.T), input_all), True)
    expand_all = lax.all_gather(
        half_of(expand_weight, part_here, core), ("narrow", "wide"), axis=0, tiled=True
    ).reshape(2, D, part_here)
    reduce_part = lax.dynamic_slice_in_dim(reduce_weight, core * part_here, part_here, 0).T
    reduce_all = gather_both(after(reduce_part, output_all))

    small = jnp.concatenate(
        [
            first_gain,
            first_shift,
            output_bias,
            second_gain,
            second_shift,
            reduce_bias,
            input_bias.reshape(-1),
            expand_bias,
        ]
    )
    small_other = side_swap(small)
    small_low = jnp.where(side == 0, small, small_other)
    small_high = jnp.where(side == 0, small_other, small)

    def full_vector(k):
        at = k * share
        return jnp.concatenate([small_low[at : at + share], small_high[at : at + share]])

    own_half = jnp.where(core == 0, small_low, small_high)
    gain_one, shift_one, bias_out, gain_two, shift_two, bias_reduce = [
        full_vector(k) for k in range(6)
    ]
    bias_in = own_half[6 * share : 8 * share].reshape(2, groups, group)
    bias_in = jnp.stack([bias_in[0], jnp.zeros_like(bias_in[0]), bias_in[1]], 1).reshape(3 * share)
    bias_expand = [half_of(v[8 * share :], part_here, core) for v in (small_low, small_high)]
    docs = turn(documents)
    starts = jnp.sum((docs[:, None, :] < docs[:, :, None]).astype(jnp.int32), -1)[:, None, :]
    residual = both_halves(turn(tokens)).astype(f32)
    upstream_low = both_halves(turn(cotangent))

    standard_one, scale_one = norm_parts(residual)
    normed_one = (standard_one * gain_one + shift_one).astype(bf16)
    projected = (dot(normed_one, input_all) + bias_in).astype(bf16)
    attended, log_sums = attend(projected, starts, group, head_dim)
    branch = dot_last(attended, output_all).astype(bf16)
    middle = residual + (branch.astype(f32) + core_swap(branch).astype(f32)) + bias_out
    standard_two, scale_two = norm_parts(middle)
    normed_two = (standard_two * gain_two + shift_two).astype(bf16)
    active, rate = [], []
    for k in range(2):
        values = gelu_parts(dot(normed_two, expand_all[k]) + bias_expand[k])
        active.append(values[0].astype(bf16))
        rate.append(values[1].astype(bf16))

    grad_reduce = jnp.concatenate([dot_first(upstream_low, active[k]).astype(bf16) for k in range(2)], 0)
    grad_reduce = lax.psum_scatter(grad_reduce, ("narrow", "wide"), scatter_dimension=0, tiled=True)
    upstream = upstream_low.astype(f32)
    grad_reduce_bias = jnp.sum(upstream, 0)
    grad_hidden = [
        (dot(upstream_low, reduce_all[k]) * rate[k].astype(f32)).astype(bf16) for k in range(2)
    ]
    branch = (dot_last(grad_hidden[0], expand_all[0]) + dot_last(grad_hidden[1], expand_all[1])).astype(bf16)
    grad_normed_two = branch.astype(f32) + core_swap(branch).astype(f32)
    grad_expand = jnp.stack([dot_first(normed_two, grad_hidden[k]).astype(bf16) for k in range(2)])
    grad_expand = scatter_both(grad_expand).astype(bf16)
    grad_expand_bias = jnp.stack([jnp.sum(grad_hidden[k].astype(f32), 0) for k in range(2)])
    grad_middle, grad_second_gain, grad_second_shift = norm_backward(
        grad_normed_two, standard_two, scale_two, gain_two
    )
    grad_middle = grad_middle + upstream
    grad_branch = grad_middle.astype(bf16)
    grad_output_bias = jnp.sum(grad_branch.astype(f32), 0)
    grad_attended = dot(grad_branch, output_all).astype(bf16)

    branch_two = (dot_last(active[0], reduce_all[0]) + dot_last(active[1], reduce_all[1])).astype(bf16)
    branch_other = core_swap(half_of(branch_two, share, 1 - core))
    layer_output = (
        half_of(middle, share, core)
        + half_of(branch_two, share, core).astype(f32)
        + branch_other.astype(f32)
        + half_of(bias_reduce, share, core)
    ).astype(bf16)
    layer_output = turn(layer_output)

    grad_output_weight = scatter_half(dot_first(grad_branch, attended).astype(bf16), True).T
    grad_projected = attend_backward(projected, starts, log_sums, grad_attended, group, head_dim)
    grad_input_weight = scatter_half(dot_first(normed_one, grad_projected).astype(bf16))
    grad_input_weight = grad_input_weight.reshape(wide_rows, groups, 3, group).transpose(0, 2, 1, 3)
    projected_sums = jnp.sum(grad_projected.astype(f32), 0).reshape(groups, 3, group)
    grad_input_bias = jnp.stack([projected_sums[:, 0].reshape(share), projected_sums[:, 2].reshape(share)])
    branch = dot_last(grad_projected, input_all).astype(bf16)
    grad_normed_one = branch.astype(f32) + core_swap(branch).astype(f32)
    grad_tokens, grad_first_gain, grad_first_shift = norm_backward(
        grad_normed_one, standard_one, scale_one, gain_one
    )
    grad_tokens = half_of(grad_tokens + grad_middle, share, core)
    grad_tokens = turn(grad_tokens.astype(bf16)).astype(f32)

    grad_reduce_weight = both_halves(grad_reduce).astype(f32).T
    grad_expand_weight = both_halves(grad_expand).astype(f32)

    def placed(values):
        blank = jnp.zeros(values.shape[:-1] + (2 * values.shape[-1],), f32)
        return lax.dynamic_update_slice_in_dim(
            blank, values, core * values.shape[-1], values.ndim - 1
        )

    def own(values):
        return placed(half_of(values, share, core))

    gathered = [
        own(grad_first_gain),
        own(grad_first_shift),
        own(grad_output_bias),
        own(grad_second_gain),
        own(grad_second_shift),
        own(grad_reduce_bias),
        placed(grad_input_bias).reshape(-1),
        placed(grad_expand_bias).reshape(-1),
    ]
    sizes = [value.shape[0] for value in gathered]
    total = all_sum(jnp.concatenate(gathered))
    sums, at = [], 0
    for size in sizes:
        sums.append(total[at : at + size])
        at += size
    sums = [half_of(value, share, side) for value in sums[:6]] + [
        half_of(sums[6].reshape(2, 2 * share), share, side),
        half_of(sums[7], hidden_half, side),
    ]
    return (
        layer_output,
        grad_tokens,
        sums[0],
        sums[1],
        grad_input_weight.reshape(-1, 3, share),
        sums[6],
        grad_output_weight,
        sums[2],
        sums[3],
        sums[4],
        grad_expand_weight,
        sums[7],
        grad_reduce_weight,
        sums[5],
    )


def solution(mesh):
    in_specs = (
        P(("dp", "wide"), "narrow"),
        P(("dp", "wide"), None),
        P("narrow"),
        P("narrow"),
        P("wide", None, "narrow"),
        P(None, "narrow"),
        P("narrow", "wide"),
        P("narrow"),
        P("narrow"),
        P("narrow"),
        P("wide", "narrow"),
        P("narrow"),
        P("narrow", "wide"),
        P("narrow"),
        P(("dp", "wide"), "narrow"),
    )
    out_specs = (
        P(("dp", "wide"), "narrow"),
        P(("dp", "wide"), "narrow"),
        P("narrow"),
        P("narrow"),
        P("wide", None, "narrow"),
        P(None, "narrow"),
        P("narrow", "wide"),
        P("narrow"),
        P("narrow"),
        P("narrow"),
        P("wide", "narrow"),
        P("narrow"),
        P("narrow", "wide"),
        P("narrow"),
    )
    return jax.shard_map(local, mesh=mesh, in_specs=in_specs, out_specs=out_specs, check_vma=False)
```

```python
import functools

import jax
import jax.numpy as jnp
from jax import lax
from jax.experimental import pallas as pl
from jax.experimental.pallas import tpu as pltpu
from jax.sharding import PartitionSpec as P

D = 1280
HEADS = 20

epsilon = 1e-05

f32 = jnp.float32
bf16 = jnp.bfloat16


def core_swap(values):
    return lax.ppermute(values, "dp", [(0, 1), (1, 0)])


def side_swap(values):
    return lax.ppermute(values, "narrow", [(0, 1), (1, 0)])


def after(values, *earlier):
    return lax.optimization_barrier((values,) + earlier)[0]


def ring_order(size):
    return list(range(0, size, 2)) + list(range(size - 1, 0, -2))


def ring_place(index, size):
    return jnp.where(index % 2 == 0, index // 2, size - 1 - index // 2)


def ring_index(place, size):
    place = place % size
    return jnp.where(place < size // 2, 2 * place, 2 * (size - 1 - place) + 1)


def ring_step(values, shift):
    size = lax.axis_size("wide")
    order = ring_order(size)
    pairs = [(order[p], order[(p + shift) % size]) for p in range(size)]
    return lax.ppermute(values, "wide", pairs)


def ring_owner(offset):
    size = lax.axis_size("wide")
    return ring_index(ring_place(lax.axis_index("wide"), size) + offset, size)


def scatter_ring(piece, flip=False):
    size = lax.axis_size("wide")
    sign = -1 if flip else 1
    total = piece(0)
    for shift, steps in ((sign, size // 2), (-sign, size - size // 2 - 1)):
        moving = None
        for step in range(steps, 0, -1):
            term = piece(shift * step)
            if moving is not None:
                term = term + moving.astype(f32)
            moving = ring_step(term.astype(bf16), shift)
        total = total + moving.astype(f32)
    return total


def gather_wide(values):
    return lax.all_gather(values, "wide", axis=0, tiled=True)


def row_halves(values):
    size = lax.axis_size("wide")
    return values.reshape(size, 2, values.shape[0] // (2 * size), values.shape[1])


def gather_rows(weight):
    core = lax.axis_index("dp")
    rows, columns = weight.shape
    half = rows // 2
    size = lax.axis_size("wide")
    mine = gather_wide(lax.dynamic_slice_in_dim(weight, core * half, half, 0))
    other = core_swap(mine)
    whole = jnp.zeros((size, 2, half, columns), weight.dtype)
    for part, at in ((mine, core), (other, 1 - core)):
        whole = lax.dynamic_update_slice(whole, part.reshape(size, 1, half, columns), (0, at, 0, 0))
    return whole.reshape(size * rows, columns)


def core_sum_rows(partial):
    core = lax.axis_index("dp")
    parts = row_halves(partial)
    shape = (parts.shape[0], 1) + parts.shape[2:]
    other = core_swap(lax.dynamic_slice(parts, (0, 1 - core, 0, 0), shape))
    total = lax.dynamic_slice(parts, (0, core, 0, 0), shape).astype(f32) + other.astype(f32)
    return total.reshape(-1, partial.shape[1]).astype(bf16)


def scatter_wide(partial):
    return lax.psum_scatter(partial, "wide", scatter_dimension=0, tiled=True)


def scatter_by_ring(partial, flip=False):
    rows = partial.shape[0] // lax.axis_size("wide")

    def piece(offset):
        return lax.dynamic_slice_in_dim(partial, ring_owner(offset) * rows, rows, 0).astype(f32)

    return scatter_ring(piece, flip).astype(bf16)


def in_order(own, other, index, axis):
    return jnp.where(
        index == 0, jnp.concatenate([own, other], axis), jnp.concatenate([other, own], axis)
    )


def half_of(values, share, index):
    return lax.dynamic_slice_in_dim(values, index * share, share, values.ndim - 1)


def side_sum(values):
    size = lax.axis_size("wide")
    if size & (size - 1):
        return lax.psum(values, ("dp", "wide"))
    total = values + core_swap(values)
    step = 1
    while step < size:
        total = total + lax.ppermute(total, "wide", [(k, k ^ step) for k in range(size)])
        step *= 2
    return total


def norm_parts(values):
    row_mean = jnp.mean(values, 1, keepdims=True)
    centred = values - row_mean
    row_var = jnp.mean(centred * centred, 1, keepdims=True)
    row_scale = lax.rsqrt(row_var + epsilon)
    return centred * row_scale, row_scale


def norm_backward(grad_in, standard, row_scale, norm_gain):
    scaled = grad_in * norm_gain
    plain = jnp.mean(scaled, 1, keepdims=True)
    cross = jnp.mean(scaled * standard, 1, keepdims=True)
    back = row_scale * (scaled - plain - standard * cross)
    return back, jnp.sum(grad_in * standard, 0), jnp.sum(grad_in, 0)


def dot_last(left, right):
    return lax.dot_general(left, right, (((1,), (1,)), ((), ())), preferred_element_type=f32)


def dot_first(left, right):
    return lax.dot_general(left, right, (((0,), (0,)), ((), ())), preferred_element_type=f32)


def dot(left, right):
    return jnp.dot(left, right, preferred_element_type=f32)


def gelu_parts(hidden):
    slope = (2.0 / 3.141592653589793) ** 0.5
    square = hidden * hidden
    bent = jnp.tanh(slope * hidden * (1.0 + 0.044715 * square))
    half = 0.5 * (1.0 + bent)
    rate = half + 0.5 * hidden * (1.0 - bent * bent) * (slope * (1.0 + 0.134145 * square))
    return hidden * half, rate


masked_value = -1e30
BLOCK = 256
REACH = 512


def key_range(block, block_rows):
    first = max(0, (block * block_rows - (REACH - 1)) // block_rows * block_rows)
    return first, (block + 1) * block_rows


def seen(starts, first, last, query_at, rows):
    keys = lax.broadcasted_iota(jnp.int32, (last - first, rows), 0) + first
    queries = lax.broadcasted_iota(jnp.int32, (last - first, rows), 1) + query_at
    return (keys <= queries) & (keys >= starts)


def attend_kernel(starts_ref, packed_ref, out_ref, logs_ref, *, head_dim):
    length = packed_ref.shape[0]
    group = out_ref.shape[1]
    rows = min(BLOCK, length)
    factor = head_dim**-0.5
    for block in range(length // rows):
        first, last = key_range(block, rows)
        at = block * rows
        allowed = seen(starts_ref[0, :, at : at + rows], first, last, at, rows)
        outs = []
        for head in range(group // head_dim):
            low = head * head_dim
            query = packed_ref[at : at + rows, low : low + head_dim] * bf16(factor)
            key = packed_ref[first:last, group + low : group + low + head_dim]
            value = packed_ref[first:last, 2 * group + low : 2 * group + low + head_dim]
            scores = lax.dot_general(key, query, (((1,), (1,)), ((), ())), preferred_element_type=f32)
            scores = jnp.where(allowed, scores, masked_value)
            top = jnp.max(scores, 0, keepdims=True)
            raised = jnp.exp(scores - top)
            total = jnp.sum(raised, 0, keepdims=True)
            mixed = lax.dot_general(
                value, raised.astype(bf16), (((0,), (0,)), ((), ())), preferred_element_type=f32
            )
            outs.append(mixed / total)
            logs_ref[0, 0, head : head + 1, at : at + rows] = top + jnp.log(total)
        out_ref[at : at + rows, :] = jnp.concatenate(outs, 0).T.astype(bf16)


def attend_backward_kernel(
    starts_ref, packed_ref, logs_ref, grad_ref, out_ref, keys_scr, values_scr, *, head_dim
):
    length = packed_ref.shape[0]
    group = grad_ref.shape[1]
    rows = min(BLOCK, length)
    factor = head_dim**-0.5
    keys_scr[...] = jnp.zeros_like(keys_scr)
    values_scr[...] = jnp.zeros_like(values_scr)
    for block in range(length // rows):
        first, last = key_range(block, rows)
        at = block * rows
        allowed = seen(starts_ref[0, :, at : at + rows], first, last, at, rows)
        queries_back = []
        keys_back = []
        values_back = []
        for head in range(group // head_dim):
            low = head * head_dim
            query = packed_ref[at : at + rows, low : low + head_dim] * bf16(factor)
            key = packed_ref[first:last, group + low : group + low + head_dim]
            value = packed_ref[first:last, 2 * group + low : 2 * group + low + head_dim]
            grad = grad_ref[at : at + rows, low : low + head_dim]
            scores = lax.dot_general(key, query, (((1,), (1,)), ((), ())), preferred_element_type=f32)
            logs = logs_ref[0, 0, head : head + 1, at : at + rows]
            probs = jnp.exp(jnp.where(allowed, scores, masked_value) - logs)
            grad_probs = lax.dot_general(
                value, grad, (((1,), (1,)), ((), ())), preferred_element_type=f32
            )
            inner = jnp.sum(probs * grad_probs, 0, keepdims=True)
            grad_scores = (probs * (grad_probs - inner)).astype(bf16)
            queries_back.append(
                lax.dot_general(key, grad_scores, (((0,), (0,)), ((), ())), preferred_element_type=f32)
            )
            keys_back.append(jnp.dot(grad_scores, query, preferred_element_type=f32))
            values_back.append(jnp.dot(probs.astype(bf16), grad, preferred_element_type=f32))
        out_ref[at : at + rows, :group] = (jnp.concatenate(queries_back, 0).T * factor).astype(bf16)
        keys_scr[first:last, :] += jnp.concatenate(keys_back, 1)
        values_scr[first:last, :] += jnp.concatenate(values_back, 1)
    out_ref[:, group : 2 * group] = keys_scr[...].astype(bf16)
    out_ref[:, 2 * group :] = values_scr[...].astype(bf16)


def attend(packed, starts, group, head_dim):
    seq_count, _, length = starts.shape
    groups = packed.shape[1] // (3 * group)
    heads = group // head_dim
    return pl.pallas_call(
        functools.partial(attend_kernel, head_dim=head_dim),
        grid=(seq_count, groups),
        in_specs=[
            pl.BlockSpec((1, 1, length), lambda s, g: (s, 0, 0)),
            pl.BlockSpec((length, 3 * group), lambda s, g: (s, g)),
        ],
        out_specs=[
            pl.BlockSpec((length, group), lambda s, g: (s, g)),
            pl.BlockSpec((1, 1, heads, length), lambda s, g: (s, g, 0, 0)),
        ],
        out_shape=[
            jax.ShapeDtypeStruct((packed.shape[0], groups * group), bf16),
            jax.ShapeDtypeStruct((seq_count, groups, heads, length), f32),
        ],
        compiler_params=pltpu.CompilerParams(vmem_limit_bytes=48 * 1024 * 1024),
        cost_estimate=pl.CostEstimate(flops=12 * 10**9, bytes_accessed=6 * 10**6, transcendentals=0),
        name="attend",
    )(starts, packed)


def attend_backward(packed, starts, logs, grad, group, head_dim):
    seq_count, _, length = starts.shape
    groups = packed.shape[1] // (3 * group)
    heads = group // head_dim
    return pl.pallas_call(
        functools.partial(attend_backward_kernel, head_dim=head_dim),
        grid=(seq_count, groups),
        in_specs=[
            pl.BlockSpec((1, 1, length), lambda s, g: (s, 0, 0)),
            pl.BlockSpec((length, 3 * group), lambda s, g: (s, g)),
            pl.BlockSpec((1, 1, heads, length), lambda s, g: (s, g, 0, 0)),
            pl.BlockSpec((length, group), lambda s, g: (s, g)),
        ],
        out_specs=pl.BlockSpec((length, 3 * group), lambda s, g: (s, g)),
        out_shape=jax.ShapeDtypeStruct(packed.shape, bf16),
        scratch_shapes=[pltpu.VMEM((length, group), f32), pltpu.VMEM((length, group), f32)],
        compiler_params=pltpu.CompilerParams(vmem_limit_bytes=48 * 1024 * 1024),
        cost_estimate=pl.CostEstimate(flops=30 * 10**9, bytes_accessed=10 * 10**6, transcendentals=0),
        name="attend_backward",
    )(starts, packed, logs, grad)


def local(
    tokens,
    documents,
    first_gain,
    first_shift,
    input_weight,
    input_bias,
    output_weight,
    output_bias,
    second_gain,
    second_shift,
    expand_weight,
    expand_bias,
    reduce_weight,
    reduce_bias,
    cotangent,
):
    token_rows, share = tokens.shape
    head_dim = D // HEADS
    group = 2 * head_dim
    groups = share // group
    hidden_here = expand_weight.shape[1]
    part = hidden_here // 2
    wide_rows = input_weight.shape[0]
    core = lax.axis_index("dp")
    side = lax.axis_index("narrow")

    small = jnp.concatenate(
        [first_gain, first_shift, output_bias, second_gain, second_shift, reduce_bias]
    )
    small_other = side_swap(small)
    gain_one, shift_one, bias_out, gain_two, shift_two, bias_reduce = [
        in_order(small[k * share : (k + 1) * share], small_other[k * share : (k + 1) * share], side, 0)
        for k in range(6)
    ]
    bias_in = input_bias.reshape(2, groups, group)
    bias_in = jnp.stack([bias_in[0], jnp.zeros_like(bias_in[0]), bias_in[1]], 1).reshape(3 * share)
    starts = jnp.sum((documents[:, None, :] < documents[:, :, None]).astype(jnp.int32), -1)[:, None, :]
    residual = in_order(tokens, side_swap(tokens), side, 1).astype(f32)
    upstream_low = in_order(cotangent, side_swap(cotangent), side, 1)

    input_rows = input_weight.reshape(wide_rows, 3, groups, group).transpose(0, 2, 1, 3)
    input_all = gather_rows(input_rows.reshape(wide_rows, 3 * share))
    output_all = gather_rows(output_weight.T)
    own_part = lax.dynamic_slice_in_dim(expand_weight, core * part, part, 1)
    expand_all = gather_wide(own_part)
    expand_all = [expand_all, core_swap(expand_all)]
    own_part = lax.dynamic_slice_in_dim(reduce_weight, core * part, part, 0).T
    reduce_all = gather_wide(own_part)
    reduce_all = [reduce_all, core_swap(reduce_all)]
    bias_expand = [half_of(expand_bias, part, core), half_of(expand_bias, part, 1 - core)]

    standard_one, scale_one = norm_parts(residual)
    normed_one = (standard_one * gain_one + shift_one).astype(bf16)
    projected = (dot(normed_one, input_all) + bias_in).astype(bf16)
    attended, log_sums = attend(projected, starts, group, head_dim)
    branch = dot_last(attended, output_all).astype(bf16)
    middle = residual + (branch.astype(f32) + side_swap(branch).astype(f32)) + bias_out
    standard_two, scale_two = norm_parts(middle)
    normed_two = (standard_two * gain_two + shift_two).astype(bf16)
    active, rate = [], []
    for k in range(2):
        values = gelu_parts(dot(normed_two, expand_all[k]) + bias_expand[k])
        active.append(values[0].astype(bf16))
        rate.append(values[1].astype(bf16))

    upstream = upstream_low.astype(f32)
    grad_reduce_bias = jnp.sum(upstream, 0)
    grad_hidden = [
        (dot(upstream_low, reduce_all[k]) * rate[k].astype(f32)).astype(bf16) for k in range(2)
    ]
    branch = (dot_last(grad_hidden[0], expand_all[0]) + dot_last(grad_hidden[1], expand_all[1])).astype(bf16)
    grad_normed_two = branch.astype(f32) + side_swap(branch).astype(f32)
    grad_feed = []
    for k in (1, 0):
        grad_feed.append(
            jnp.concatenate(
                [
                    dot_first(normed_two, grad_hidden[k]).astype(bf16),
                    dot_first(upstream_low, active[k]).astype(bf16),
                ],
                1,
            )
        )
    grad_feed = (grad_feed[1].astype(f32) + core_swap(grad_feed[0]).astype(f32)).astype(bf16)
    grad_feed = scatter_wide(grad_feed)
    grad_expand_bias = jnp.concatenate([jnp.sum(grad_hidden[k].astype(f32), 0) for k in range(2)])
    grad_expand_bias = in_order(grad_expand_bias[:part], grad_expand_bias[part:], core, 0)
    grad_middle, grad_second_gain, grad_second_shift = norm_backward(
        grad_normed_two, standard_two, scale_two, gain_two
    )
    grad_middle = grad_middle + upstream
    grad_branch = grad_middle.astype(bf16)
    grad_output_bias = jnp.sum(grad_branch.astype(f32), 0)
    grad_attended = dot(grad_branch, output_all).astype(bf16)

    branch = (dot_last(active[0], reduce_all[0]) + dot_last(active[1], reduce_all[1])).astype(bf16)
    branch_other = side_swap(half_of(branch, share, 1 - side))
    layer_output = (
        half_of(middle, share, side)
        + (half_of(branch, share, side).astype(f32) + branch_other.astype(f32))
        + reduce_bias
    ).astype(bf16)

    grad_output = dot_first(grad_branch, attended).astype(bf16)
    grad_projected = attend_backward(projected, starts, log_sums, grad_attended, group, head_dim)
    grad_input = dot_first(normed_one, grad_projected).astype(bf16)
    grad_near = jnp.concatenate([core_sum_rows(grad_input), core_sum_rows(grad_output)], 1)
    grad_near = scatter_by_ring(grad_near)
    projected_sums = jnp.sum(grad_projected.astype(f32), 0).reshape(groups, 3, group)
    grad_input_bias = jnp.stack([projected_sums[:, 0].reshape(share), projected_sums[:, 2].reshape(share)])
    branch = dot_last(grad_projected, input_all).astype(bf16)
    grad_normed_one = half_of(branch, share, side).astype(f32) + side_swap(
        half_of(branch, share, 1 - side)
    ).astype(f32)
    standard_half = half_of(standard_one, share, side)
    scaled = grad_normed_one * first_gain
    sums = jnp.stack([jnp.sum(scaled, 1), jnp.sum(scaled * standard_half, 1)])
    sums = (sums + side_swap(sums)) / D
    grad_tokens = half_of(grad_middle, share, side) + scale_one * (
        scaled - sums[0][:, None] - standard_half * sums[1][:, None]
    )
    grad_first_gain = jnp.sum(grad_normed_one * standard_half, 0)
    grad_first_shift = jnp.sum(grad_normed_one, 0)

    settled = jnp.concatenate([grad_near, grad_feed.reshape(grad_near.shape[0], -1)], 1)
    settled_other = core_swap(settled)
    near_columns = grad_near.shape[1]
    grad_near = in_order(settled[:, :near_columns], settled_other[:, :near_columns], core, 0).astype(f32)
    grad_feed_other = settled_other[:, near_columns:].reshape(wide_rows, 2 * part)
    grad_expand_weight = in_order(grad_feed[:, :part], grad_feed_other[:, :part], core, 1).astype(f32)
    grad_reduce_weight = in_order(grad_feed[:, part:], grad_feed_other[:, part:], core, 1).astype(f32).T
    grad_input_weight = grad_near[:, : 3 * share].reshape(wide_rows, groups, 3, group).transpose(0, 2, 1, 3)
    grad_output_weight = grad_near[:, 3 * share :].T

    gathered = [
        grad_first_gain,
        grad_first_shift,
        half_of(grad_output_bias, share, side),
        half_of(grad_second_gain, share, side),
        half_of(grad_second_shift, share, side),
        half_of(grad_reduce_bias, share, side),
        grad_input_bias.reshape(-1),
        grad_expand_bias,
    ]
    sizes = [value.shape[0] for value in gathered]
    total = side_sum(jnp.concatenate(gathered))
    sums, at = [], 0
    for size in sizes:
        sums.append(total[at : at + size])
        at += size
    return (
        layer_output,
        grad_tokens,
        sums[0],
        sums[1],
        grad_input_weight.reshape(-1, 3, share),
        sums[6].reshape(2, share),
        grad_output_weight,
        sums[2],
        sums[3],
        sums[4],
        grad_expand_weight,
        sums[7],
        grad_reduce_weight,
        sums[5],
    )


def solution(mesh):
    in_specs = (
        P(("dp", "wide"), "narrow"),
        P(("dp", "wide"), None),
        P("narrow"),
        P("narrow"),
        P("wide", None, "narrow"),
        P(None, "narrow"),
        P("narrow", "wide"),
        P("narrow"),
        P("narrow"),
        P("narrow"),
        P("wide", "narrow"),
        P("narrow"),
        P("narrow", "wide"),
        P("narrow"),
        P(("dp", "wide"), "narrow"),
    )
    out_specs = (
        P(("dp", "wide"), "narrow"),
        P(("dp", "wide"), "narrow"),
        P("narrow"),
        P("narrow"),
        P("wide", None, "narrow"),
        P(None, "narrow"),
        P("narrow", "wide"),
        P("narrow"),
        P("narrow"),
        P("narrow"),
        P("wide", "narrow"),
        P("narrow"),
        P("narrow", "wide"),
        P("narrow"),
    )
    return jax.shard_map(local, mesh=mesh, in_specs=in_specs, out_specs=out_specs, check_vma=False)
```
